32 devices in a mesh: frame: 8 (over z, core), row: 4 (over y, x).
Axes of the slice: x: 2, y: 2, z: 4, core: 2. Of those that a mesh axis runs over, the one named last changes fastest.
Arguments:
- queries: bfloat16 [16, 16, 64, 2240], P('frame', 'row'), may hold values from -6 to 6
- keys: bfloat16 [16, 16, 64, 2240], P('frame', 'row'), may hold values from -12 to 12
- values: bfloat16 [16, 16, 64, 2240], P('frame', 'row'), may hold values from -12 to 12
- gate: bfloat16 [16, 16, 64, 2240], P('frame', 'row'), may hold values from -8 to 8
- conv_weight: float32 [3, 3, 2240], replicated, may hold values from -2 to 2
Outputs:
- mixed: bfloat16 [16, 16, 64, 2240], P('frame', 'row')
The draws below stay inside these ranges and needn't reach their ends.
All inputs are finite; a program needn't handle non-finite values.
Results may differ from the reference program's by a relative error of at most 0.005.
Values may be sent and summed in bfloat16 or wider, within the bound.
No kernel may reach another device: no remote copies, remote signals or barrier semaphores. Data moves between devices by JAX's collectives and lax.ppermute only.
A program may use at most 128 MiB of HBM per device.

```python
import jax
import jax.numpy as jnp
from jax import lax

HEADS = 70
HEAD_DIM = 32
D = 2240
WIDTH = 64
FRAMES = 16
ROWS = 16


def draw_keys(key, part):
    shape = (FRAMES, ROWS, WIDTH, HEADS * HEAD_DIM)
    rise = 1.0 + 2.0 * jnp.arange(FRAMES, dtype=jnp.float32) / (FRAMES - 1)
    base = jnp.clip(jax.random.normal(jax.random.fold_in(key, 11), shape, jnp.float32), -4.0, 4.0)
    return jnp.clip(base * rise[:, None, None, None], -12.0, 12.0).astype(jnp.bfloat16)


def draw_values(key, part):
    shape = (FRAMES, ROWS, WIDTH, HEADS * HEAD_DIM)
    noise = jax.random.normal(jax.random.fold_in(key, 21), shape, jnp.float32)
    offset = 3.0 * jax.random.normal(jax.random.fold_in(key, 22), (FRAMES, ROWS, 1, HEADS * HEAD_DIM), jnp.float32)
    return jnp.clip(noise + offset, -12.0, 12.0).astype(jnp.bfloat16)


def block_levels(stream_key, shape, cuts, low, largest):
    level = 1.0
    for position, parts in cuts:
        steps = jax.random.uniform(jax.random.fold_in(jax.random.fold_in(stream_key, 6), position), (parts,), jnp.float32, low / len(cuts), largest / len(cuts))
        level = level * jnp.repeat(jnp.exp(steps), shape[position] // parts).reshape((-1,) + (1,) * (len(shape) - 1 - position))
    return level


def gaussian(own_key, extent, width, bound, split=(), kind=jnp.bfloat16):
    array = width * jax.random.normal(own_key, extent, jnp.float32)
    if split:
        array = array * block_levels(own_key, extent, split, -0.22, 0.18)
    return jnp.clip(array, -bound, bound).astype(kind)


def setup_inputs(seed: int = 0) -> dict:
    arg_keys = jax.random.split(jax.random.key(seed), 6)
    queries = gaussian(arg_keys[0], (FRAMES, ROWS, WIDTH, D), 1.0, 6.0, ((0, 8), (1, 4)))
    keys = draw_keys(jax.random.fold_in(arg_keys[5], 71), 0)
    values = draw_values(jax.random.fold_in(arg_keys[5], 71), 0)
    gate = gaussian(arg_keys[3], (FRAMES, ROWS, WIDTH, D), 1.5, 8.0, ((0, 8), (1, 4)))
    conv_weight = gaussian(arg_keys[4], (3, 3, D), 9 ** -0.5, 2.0, (), jnp.float32)
    return {"queries": queries, "keys": keys, "values": values, "gate": gate, "conv_weight": conv_weight}


def frame_sums(pair):
    keyf, valf = pair
    kf = jax.nn.relu(keyf).astype(jnp.float32).reshape(ROWS * WIDTH, HEADS, HEAD_DIM)
    vf = valf.astype(jnp.float32).reshape(ROWS * WIDTH, HEADS, HEAD_DIM)
    partial_value = jnp.einsum("thd,the->hde", kf, vf, precision=lax.Precision.HIGHEST)
    return partial_value, jnp.sum(kf, axis=0)


def frame_out(items):
    query, states, zsum, gatef, conv_weight = items
    qf = jax.nn.relu(query).astype(jnp.float32).reshape(ROWS * WIDTH, HEADS, HEAD_DIM)
    numer = jnp.einsum("thd,hde->the", qf, states, precision=lax.Precision.HIGHEST)
    denom = jnp.einsum("thd,hd->th", qf, zsum, precision=lax.Precision.HIGHEST)
    attended = (numer / (denom[:, :, None] + 1e-6)).reshape(ROWS, WIDTH, HEADS * HEAD_DIM).astype(jnp.bfloat16)
    padded = jnp.pad(attended, ((1, 1), (1, 1), (0, 0))).astype(jnp.float32)
    conv = jnp.zeros((ROWS, WIDTH, HEADS * HEAD_DIM), jnp.float32)
    for a in range(3):
        for b in range(3):
            conv = conv + conv_weight[a, b] * padded[a:a + ROWS, b:b + WIDTH]
    return (conv * jax.nn.silu(gatef.astype(jnp.float32))).astype(jnp.bfloat16)


def reference(queries, keys, values, gate, conv_weight):
    partial_value, norm_part = lax.map(frame_sums, (keys, values))
    states = jnp.cumsum(partial_value, axis=0)
    zsum = jnp.cumsum(norm_part, axis=0)
    weights = jnp.broadcast_to(conv_weight, (queries.shape[0],) + conv_weight.shape)
    return lax.map(frame_out, (queries, states, zsum, gate, weights))
```

```python
import functools

import jax
import jax.numpy as jnp
from jax import lax
from jax.experimental import pallas as pl
from jax.experimental.pallas import tpu as pltpu
from jax.sharding import PartitionSpec as P

HEAD_DIM = 32
LANES = 128
GROUP = LANES // HEAD_DIM
Z_ALIGN = 16


def ceil_div(a, b):
    return -(-a // b)


class Plan:
    def __init__(self, channels, halves):
        total = ceil_div(channels, LANES)
        self.channels = channels
        self.halves = halves
        self.blocks = ceil_div(total, halves)
        self.per = max(p for p in (1, 2, 3) if self.blocks % p == 0)
        self.steps = self.blocks // self.per
        self.z_row = self.blocks * HEAD_DIM
        self.rows = self.z_row + ceil_div(self.blocks, Z_ALIGN) * Z_ALIGN
        self.width = self.per * LANES


def same_head():
    row = lax.broadcasted_iota(jnp.int32, (LANES, LANES), 0) // HEAD_DIM
    col = lax.broadcasted_iota(jnp.int32, (LANES, LANES), 1) // HEAD_DIM
    return row == col


def sums_kernel(plan, frames, half_ref, k_ref, v_ref, o_ref, acc_ref):
    step = pl.program_id(0)
    mask = same_head()

    @pl.when(step == 0)
    def _():
        acc_ref[:, plan.z_row :, :] = jnp.zeros(
            (frames, plan.rows - plan.z_row, LANES), jnp.float32
        )

    for f in range(frames):
        for b in range(plan.per):
            lanes = slice(b * LANES, (b + 1) * LANES)
            kf = jnp.maximum(k_ref[f, :, lanes], 0)
            full = lax.dot_general(
                kf,
                v_ref[f, :, lanes],
                (((0,), (0,)), ((), ())),
                preferred_element_type=jnp.float32,
            )
            full = jnp.where(mask, full, 0.0)
            state = full.reshape(GROUP, HEAD_DIM, LANES).sum(axis=0)
            norm = jnp.sum(kf.astype(jnp.float32), axis=0, keepdims=True)
            block = step * plan.per + b
            acc_ref[f, pl.ds(pl.multiple_of(block * HEAD_DIM, HEAD_DIM), HEAD_DIM), :] = state
            acc_ref[f, pl.ds(plan.z_row + block, 1), :] = norm

    @pl.when(step == plan.steps - 1)
    def _():
        o_ref[...] = acc_ref[...].astype(o_ref.dtype)


def sums(plan, half, keys, values, dtype):
    frames, tokens, _ = keys.shape
    block = pl.BlockSpec(
        (frames, tokens, plan.width), lambda i, half: (0, 0, half[0] * plan.steps + i)
    )
    return pl.pallas_call(
        functools.partial(sums_kernel, plan, frames),
        grid_spec=pltpu.PrefetchScalarGridSpec(
            num_scalar_prefetch=1,
            grid=(plan.steps,),
            in_specs=[block, block],
            out_specs=pl.BlockSpec(
                (frames, plan.rows, LANES), lambda i, half: (0, 0, 0)
            ),
            scratch_shapes=[pltpu.VMEM((frames, plan.rows, LANES), jnp.float32)],
        ),
        out_shape=jax.ShapeDtypeStruct((frames, plan.rows, LANES), dtype),
        compiler_params=pltpu.CompilerParams(
            dimension_semantics=("arbitrary",), vmem_limit_bytes=32 << 20
        ),
        cost_estimate=pl.CostEstimate(
            flops=2 * frames * tokens * plan.blocks * LANES * LANES,
            bytes_accessed=4 * frames * tokens * plan.blocks * LANES,
            transcendentals=0,
        ),
        name="sums",
    )(half, keys, values)


def mix_kernel(plan, shape, half_ref, s_ref, q_ref, up_ref, down_ref, g_ref, w_ref, *rest):
    o_ref = rest[-1]
    frames, rows, width = shape
    step = pl.program_id(0)
    mask = same_head()
    ones = mask.astype(jnp.bfloat16)
    eye = lax.broadcasted_iota(jnp.int32, (LANES, LANES), 0) == lax.broadcasted_iota(
        jnp.int32, (LANES, LANES), 1
    )
    z_rows = plan.rows - plan.z_row
    z_iota = lax.broadcasted_iota(jnp.int32, (z_rows, LANES), 0)
    lane = lax.broadcasted_iota(jnp.int32, (1, LANES), 1)
    col = lax.broadcasted_iota(jnp.int32, (rows, width, LANES), 1)
    first = (half_ref[0] * plan.steps + step) * plan.width
    for f in range(frames):
        zs = s_ref[f, plan.z_row :, :].astype(jnp.float32)
        for b in range(plan.per):
            lanes = slice(b * LANES, (b + 1) * LANES)
            block = step * plan.per + b
            live = lane + (first + b * LANES) < plan.channels
            state = s_ref[f, pl.ds(pl.multiple_of(block * HEAD_DIM, HEAD_DIM), HEAD_DIM), :]
            tiled = jnp.concatenate([state.astype(jnp.float32)] * GROUP, axis=0)
            numer_w = jnp.where(mask & live, tiled, 0.0).astype(jnp.bfloat16)
            z = jnp.sum(jnp.where(z_iota == block, zs, 0.0), axis=0, keepdims=True)
            z = jnp.where(live, z, 0.0)
            diag = jnp.where(eye, z, 0.0).astype(jnp.bfloat16)
            denom_w = jnp.dot(diag, ones, preferred_element_type=jnp.float32).astype(jnp.bfloat16)
            weights = jnp.concatenate([numer_w, denom_w], axis=1)
            q = jnp.concatenate(
                [
                    up_ref[f, :, :, lanes].reshape(width, LANES),
                    q_ref[f, :, :, lanes].reshape(rows * width, LANES),
                    down_ref[f, :, :, lanes].reshape(width, LANES),
                ],
                axis=0,
            )
            qf = jnp.where(live, jnp.maximum(q, 0), jnp.zeros_like(q))
            both = jnp.dot(qf, weights, preferred_element_type=jnp.float32)
            att = both[:, :LANES] / (both[:, LANES:] + 1e-6)
            att = att.astype(jnp.bfloat16).astype(jnp.float32)
            att = att.reshape(rows + 2, width, LANES)
            mixes = []
            for c in range(3):
                total = att[0:rows] * w_ref[c, lanes]
                for a in range(1, 3):
                    total = total + att[a : a + rows] * w_ref[3 * a + c, lanes]
                mixes.append(total)
            conv = mixes[1]
            conv = conv + jnp.where(col == 0, 0.0, pltpu.roll(mixes[0], 1, axis=1))
            conv = conv + jnp.where(
                col == width - 1, 0.0, pltpu.roll(mixes[2], width - 1, axis=1)
            )
            g = g_ref[f, :, :, lanes].astype(jnp.float32)
            o_ref[f, :, :, lanes] = (conv * g / (1.0 + jnp.exp(-g))).astype(o_ref.dtype)


def mix(plan, half, states, queries, up, down, gate, weight, earlier):
    frames, rows, width, channels = queries.shape
    col = lambda i, half: (0, 0, 0, half[0] * plan.steps + i)
    body = pl.BlockSpec((frames, rows, width, plan.width), col)
    edge = pl.BlockSpec((frames, 1, width, plan.width), col)
    in_specs = [
        pl.BlockSpec((frames, plan.rows, LANES), lambda i, half: (0, 0, 0)),
        body,
        edge,
        edge,
        body,
        pl.BlockSpec((9, plan.width), lambda i, half: (0, half[0] * plan.steps + i)),
    ]
    operands = [states, queries, up, down, gate, weight]
    aliases = {}
    if earlier is not None:
        in_specs.append(pl.BlockSpec(memory_space=pl.ANY))
        operands.append(earlier)
        aliases = {7: 0}
    tokens = frames * (rows + 2) * width
    return pl.pallas_call(
        functools.partial(mix_kernel, plan, (frames, rows, width)),
        grid_spec=pltpu.PrefetchScalarGridSpec(
            num_scalar_prefetch=1,
            grid=(plan.steps,),
            in_specs=in_specs,
            out_specs=body,
        ),
        out_shape=jax.ShapeDtypeStruct(queries.shape, jnp.bfloat16),
        input_output_aliases=aliases,
        compiler_params=pltpu.CompilerParams(
            dimension_semantics=("arbitrary",), vmem_limit_bytes=32 << 20
        ),
        cost_estimate=pl.CostEstimate(
            flops=2 * tokens * plan.blocks * LANES * LANES * 2,
            bytes_accessed=8 * tokens * plan.blocks * LANES,
            transcendentals=tokens * plan.blocks * LANES,
        ),
        name="mix",
    )(half, *operands)


def swap(array, axis, bit):
    n = lax.axis_size(axis)
    return lax.ppermute(array, axis, [(i, i ^ bit) for i in range(n)])


def per_device(queries, keys, values, gate, conv_weight):
    frames, rows, width, channels = queries.shape
    tokens = rows * width
    n_row, n_frame = lax.axis_size("row"), lax.axis_size("frame")
    me_row, me_frame = lax.axis_index("row"), lax.axis_index("frame")
    f32, bf16 = jnp.float32, jnp.bfloat16

    top = n_row // 2
    plan = Plan(channels, 2)
    own = (me_row // top).astype(jnp.int32).reshape(1)
    other = 1 - own

    ring = [(i, i + 1) for i in range(n_row - 1)]
    up = lax.ppermute(queries[:, rows - 1 :], "row", ring)
    down = lax.ppermute(queries[:, :1], "row", [(j, i) for i, j in ring])

    keys = keys.reshape(frames, tokens, channels)
    values = values.reshape(frames, tokens, channels)
    send = sums(plan, other, keys, values, bf16)
    got = swap(send, "row", top)
    mine = sums(plan, own, keys, values, f32) + got.astype(f32)

    total = jnp.sum(mine, axis=0)
    neighbour = swap(total.astype(bf16), "frame", 1).astype(f32)
    second = (me_frame % 2) == 1
    before = jnp.where(second, neighbour, 0.0)
    running = total + neighbour
    pairs = n_frame // 2
    reach = 1
    while reach < pairs:
        hop = [(i, i + 2 * reach) for i in range(n_frame - 2 * reach)]
        earlier = lax.ppermute(running.astype(bf16), "frame", hop).astype(f32)
        before = before + earlier
        running = running + earlier
        reach *= 2
    states = before[None] + jnp.cumsum(mine, axis=0)
    bit = 1
    while bit < top:
        states = states + swap(states.astype(bf16), "row", bit).astype(f32)
        bit *= 2
    states = states.astype(bf16)
    others = swap(states, "row", top)

    weight = conv_weight.reshape(9, channels)
    out = mix(plan, own, states, queries, up, down, gate, weight, None)
    return mix(plan, other, others, queries, up, down, gate, weight, out)


def solution(mesh):
    spec = P("frame", "row", None, None)
    return jax.shard_map(
        per_device,
        mesh=mesh,
        in_specs=(spec, spec, spec, spec, P()),
        out_specs=spec,
        check_vma=False,
    )
```

```python
import functools

import jax
import jax.numpy as jnp
from jax import lax
from jax.experimental import pallas as pl
from jax.experimental.pallas import tpu as pltpu
from jax.sharding import PartitionSpec as P

HEAD_DIM = 32
LANES = 128
GROUP = LANES // HEAD_DIM
Z_ALIGN = 16
MARGIN = 8
CHUNK = 16
PARTS = 2
SUMS_LIMIT = 60 << 20
READY_LIMIT = 52 << 20
MIX_LIMIT = 40 << 20


def ceil_div(a, b):
    return -(-a // b)


class Plan:
    def __init__(self, channels, halves):
        total = ceil_div(channels, LANES)
        self.channels = channels
        self.halves = halves
        self.blocks = ceil_div(total, halves)
        self.per = max(p for p in (1, 2, 3) if self.blocks % p == 0)
        self.steps = self.blocks // self.per
        self.z_row = self.blocks * HEAD_DIM
        self.rows = self.z_row + ceil_div(self.blocks, Z_ALIGN) * Z_ALIGN
        self.width = self.per * LANES


def same_head():
    row = lax.broadcasted_iota(jnp.int32, (LANES, LANES), 0) // HEAD_DIM
    col = lax.broadcasted_iota(jnp.int32, (LANES, LANES), 1) // HEAD_DIM
    return row == col


def sums_kernel(
    plan,
    own_ref,
    odd_ref,
    k_hbm,
    v_hbm,
    q_hbm,
    send_ref,
    mine_ref,
    far_ref,
    *rest,
):
    *near_refs, k_ref, v_ref, acc_ref, sems, edge_sems = rest
    frames, tokens, channels = k_ref.shape
    rows = q_hbm.shape[1]
    part = tokens // PARTS
    odd = odd_ref[0]
    copies = []
    for f in range(frames):
        for p in range(PARTS):
            at = (f, pl.ds(p * part, part))
            copies.append(
                [
                    pltpu.make_async_copy(k_hbm.at[at], k_ref.at[at], sems.at[0, f, p]),
                    pltpu.make_async_copy(v_hbm.at[at], v_ref.at[at], sems.at[1, f, p]),
                ]
            )
    edges = [
        pltpu.make_async_copy(
            q_hbm.at[:, pl.ds((rows - 1) * (1 - odd), 1)], near, edge_sems.at[f]
        )
        for f, near in enumerate(near_refs)
    ]
    edges.append(
        pltpu.make_async_copy(
            q_hbm.at[:, pl.ds((rows - 1) * odd, 1)], far_ref, edge_sems.at[1]
        )
    )
    for pair in copies:
        for copy in pair:
            copy.start()
    for edge in edges:
        edge.start()

    mask = same_head()
    acc_ref[:, :, plan.z_row :, :] = jnp.zeros(
        (plan.halves, frames, plan.rows - plan.z_row, LANES), jnp.float32
    )
    for f in range(frames):
        for pair in copies[f * PARTS : (f + 1) * PARTS]:
            for copy in pair:
                copy.wait()
        for index in range(ceil_div(channels, LANES)):
            half, block = divmod(index, plan.blocks)
            lanes = slice(index * LANES, min((index + 1) * LANES, channels))
            kf = jnp.maximum(k_ref[f, :, lanes], 0)
            v = v_ref[f, :, lanes]
            if kf.shape[1] < LANES:
                rest = jnp.zeros((tokens, LANES - kf.shape[1]), kf.dtype)
                kf = jnp.concatenate([kf, rest], axis=1)
                v = jnp.concatenate([v, rest], axis=1)
            full = lax.dot_general(
                kf, v, (((0,), (0,)), ((), ())), preferred_element_type=jnp.float32
            )
            full = jnp.where(mask, full, 0.0)
            state = full.reshape(GROUP, HEAD_DIM, LANES).sum(axis=0)
            norm = jnp.sum(kf.astype(jnp.float32), axis=0, keepdims=True)
            acc_ref[half, f, block * HEAD_DIM : (block + 1) * HEAD_DIM, :] = state
            acc_ref[half, f, plan.z_row + block : plan.z_row + block + 1, :] = norm
    own = own_ref[0]
    mine_ref[...] = acc_ref[own]
    send_ref[...] = acc_ref[1 - own].astype(send_ref.dtype)
    for edge in edges:
        edge.wait()


def sums(plan, own, odd, keys, values, queries):
    frames, tokens, channels = keys.shape
    _, rows, width, _ = queries.shape
    scalar = pl.BlockSpec(memory_space=pltpu.SMEM)
    anywhere = pl.BlockSpec(memory_space=pl.ANY)
    whole = pl.BlockSpec(memory_space=pltpu.VMEM)
    state = (frames, plan.rows, LANES)
    return pl.pallas_call(
        functools.partial(sums_kernel, plan),
        in_specs=[scalar, scalar, anywhere, anywhere, anywhere],
        out_specs=[whole] * 4,
        scratch_shapes=[
            pltpu.VMEM((frames, tokens, channels), keys.dtype),
            pltpu.VMEM((frames, tokens, channels), values.dtype),
            pltpu.VMEM((plan.halves, frames, plan.rows, LANES), jnp.float32),
            pltpu.SemaphoreType.DMA((2, frames, PARTS)),
            pltpu.SemaphoreType.DMA((2,)),
        ],
        out_shape=[
            pltpu.VMEM(state, jnp.bfloat16),
            pltpu.VMEM(state, jnp.float32),
            pltpu.VMEM((frames, 1, width, channels), queries.dtype),
        ]
        + [pltpu.VMEM((frames, 1, width, channels), queries.dtype)],
        compiler_params=pltpu.CompilerParams(vmem_limit_bytes=SUMS_LIMIT),
        cost_estimate=pl.CostEstimate(
            flops=2 * frames * tokens * channels * LANES,
            bytes_accessed=4 * frames * tokens * channels,
            transcendentals=0,
        ),
        name="sums",
    )(own, odd, keys, values, queries)


def ready_kernel(plan, q_ref, g_ref, qf_ref, sg_ref):
    step = pl.program_id(0)
    frames, tokens = qf_ref.shape[1:3]
    lane = lax.broadcasted_iota(jnp.int32, (1, LANES), 1)
    for b in range(plan.per):
        lanes = slice(b * LANES, (b + 1) * LANES)
        block = step * plan.per + b
        live = lane + block * LANES < plan.channels
        q = q_ref[:, :, :, lanes].reshape(frames, tokens, LANES)
        qf_ref[block] = jnp.where(live, jnp.maximum(q, 0), jnp.zeros_like(q))
        g = 0.5 * g_ref[:, :, :, lanes].astype(jnp.float32).reshape(frames, tokens, LANES)
        sg_ref[block] = g + g * jnp.tanh(g)


def ready(plan, queries, gate):
    frames, rows, width, channels = queries.shape
    body = pl.BlockSpec((frames, rows, width, plan.width), lambda i: (0, 0, 0, i))
    whole = pl.BlockSpec(memory_space=pltpu.VMEM)
    shape = (plan.halves * plan.blocks, frames, rows * width, LANES)
    return pl.pallas_call(
        functools.partial(ready_kernel, plan),
        grid=(plan.halves * plan.steps,),
        in_specs=[body, body],
        out_specs=[whole, whole],
        out_shape=[pltpu.VMEM(shape, jnp.bfloat16), pltpu.VMEM(shape, jnp.float32)],
        compiler_params=pltpu.CompilerParams(
            dimension_semantics=("arbitrary",), vmem_limit_bytes=READY_LIMIT
        ),
        cost_estimate=pl.CostEstimate(
            flops=8 * frames * rows * width * channels,
            bytes_accessed=10 * frames * rows * width * channels,
            transcendentals=frames * rows * width * channels,
        ),
        name="ready",
    )(queries, gate)


def mix_kernel(plan, shape, half_ref, odd_ref, s_ref, qf_ref, sg_ref, w_ref, far_ref, *rest):
    o_ref, att_ref = rest[-2:]
    near_ref = rest[0]
    frames, rows, width = shape
    step = pl.program_id(0)
    ones = same_head().astype(jnp.bfloat16)
    nothing = jnp.zeros_like(ones)
    lower = jnp.concatenate([nothing, ones], axis=1)
    z_iota = lax.broadcasted_iota(jnp.int32, (plan.rows - plan.z_row, LANES), 0)
    lane = lax.broadcasted_iota(jnp.int32, (1, LANES), 1)
    first = (half_ref[0] * plan.steps + step) * plan.width

    half_block = half_ref[0] * plan.blocks
    near_row = (rows + 1) * (1 - odd_ref[0])

    @pl.when(step == 0)
    def _():
        side = jnp.zeros(att_ref.shape[:2] + (MARGIN, LANES), jnp.float32)
        att_ref[:, :, :MARGIN, :] = side
        att_ref[:, :, MARGIN + width :, :] = side

    for f in range(frames):
        zs = s_ref[f, plan.z_row :, :].astype(jnp.float32)
        for b in range(plan.per):
            slot = (f * plan.per + b) % att_ref.shape[0]
            lanes = slice(b * LANES, (b + 1) * LANES)
            block = step * plan.per + b
            live = lane + (first + b * LANES) < plan.channels
            state = s_ref[f, pl.ds(pl.multiple_of(block * HEAD_DIM, HEAD_DIM), HEAD_DIM), :]
            numer = jnp.concatenate([state] * GROUP, axis=0) * ones
            weights = jnp.concatenate(
                [jnp.concatenate([numer, nothing], axis=1), lower], axis=0
            )
            z = jnp.sum(jnp.where(z_iota == block, zs, 0.0), axis=0, keepdims=True)
            z = z.astype(jnp.bfloat16)
            edge = jnp.concatenate(
                [
                    near_ref[f, :, :, lanes].reshape(width, LANES),
                    far_ref[f, :, :, lanes].reshape(width, LANES),
                ],
                axis=0,
            )
            edge = jnp.where(live, jnp.maximum(edge, 0), jnp.zeros_like(edge))
            qf = jnp.concatenate([qf_ref[half_block + block, f], edge], axis=0)
            both = jnp.dot(
                jnp.concatenate([qf, qf * z], axis=1),
                weights,
                preferred_element_type=jnp.float32,
            )
            att = both[:, :LANES] * pltpu.reciprocal(both[:, LANES:] + 1e-6, approx=True)
            att = att.reshape(rows + 2, width, LANES)
            att_ref[slot, 1 : rows + 1, MARGIN : MARGIN + width, :] = att[:rows]
            att_ref[slot, near_row, MARGIN : MARGIN + width, :] = att[rows]
            att_ref[slot, rows + 1 - near_row, MARGIN : MARGIN + width, :] = att[rows + 1]
            taps = [[w_ref[a, c, lanes] for c in range(3)] for a in range(3)]
            for start in range(0, width, CHUNK):
                near = [
                    [
                        att_ref[slot, r, pl.ds(MARGIN - 1 + c + start, CHUNK), :]
                        for c in range(3)
                    ]
                    for r in range(rows + 2)
                ]
                for r in range(rows):
                    conv = None
                    for a in range(3):
                        for c in range(3):
                            term = near[r + a][c] * taps[a][c]
                            conv = term if conv is None else conv + term
                    at = r * width + start
                    mixed = conv * sg_ref[half_block + block, f, at : at + CHUNK, :]
                    o_ref[f, r, start : start + CHUNK, lanes] = mixed.astype(o_ref.dtype)


def mix(plan, shape, half, odd, states, qf, near, far, sg, weight, earlier):
    frames, rows, width, channels = shape
    col = lambda i, half, odd: (0, 0, 0, half[0] * plan.steps + i)
    body = pl.BlockSpec((frames, rows, width, plan.width), col)
    edge = lambda n: pl.BlockSpec((n, 1, width, plan.width), col)
    whole = pl.BlockSpec(memory_space=pltpu.VMEM)
    in_specs = [
        whole,
        whole,
        whole,
        pl.BlockSpec((3, 3, plan.width), lambda i, half, odd: (0, 0, half[0] * plan.steps + i)),
        edge(frames),
        edge(frames),
    ]
    operands = [states, qf, sg, weight, far, *near]
    aliases = {}
    if earlier is not None:
        in_specs.append(pl.BlockSpec(memory_space=pl.ANY))
        operands.append(earlier)
        aliases = {8: 0}
    tokens = frames * (rows + 2) * width
    return pl.pallas_call(
        functools.partial(mix_kernel, plan, (frames, rows, width)),
        grid_spec=pltpu.PrefetchScalarGridSpec(
            num_scalar_prefetch=2,
            grid=(plan.steps,),
            in_specs=in_specs,
            out_specs=body,
            scratch_shapes=[
                pltpu.VMEM((2, rows + 2, width + 2 * MARGIN, LANES), jnp.float32)
            ],
        ),
        out_shape=jax.ShapeDtypeStruct(shape, jnp.bfloat16),
        input_output_aliases=aliases,
        compiler_params=pltpu.CompilerParams(
            dimension_semantics=("arbitrary",), vmem_limit_bytes=MIX_LIMIT
        ),
        cost_estimate=pl.CostEstimate(
            flops=2 * tokens * plan.blocks * LANES * LANES * 2,
            bytes_accessed=8 * tokens * plan.blocks * LANES,
            transcendentals=tokens * plan.blocks * LANES,
        ),
        name="mix",
    )(half, odd, *operands)


def swap(array, axis, bit):
    n = lax.axis_size(axis)
    return lax.ppermute(array, axis, [(i, i ^ bit) for i in range(n)])


def cross(edge):
    n_row, n_frame = lax.axis_size("row"), lax.axis_size("frame")
    pairs = [(i, i + 1) for i in range(1, n_row - 1, 2)]
    pairs = pairs + [(j, i) for i, j in pairs]
    if n_row != 4 or n_frame % 2:
        return lax.ppermute(edge, "row", pairs), lambda held: held
    both = ("frame", "row")
    one, two = [], []
    for f in range(n_frame):
        for i, j in pairs:
            corner = i ^ 2
            if f % 2:
                one.append((f * n_row + i, f * n_row + corner))
                two.append((f * n_row + corner, f * n_row + j))
            else:
                one.append((f * n_row + i, f * n_row + j))
                two.append((f * n_row + j, f * n_row + j))
    return lax.ppermute(edge, both, one), lambda held: lax.ppermute(held, both, two)


def per_device(queries, keys, values, gate, conv_weight):
    frames, rows, width, channels = queries.shape
    tokens = rows * width
    n_row, n_frame = lax.axis_size("row"), lax.axis_size("frame")
    me_row, me_frame = lax.axis_index("row"), lax.axis_index("frame")
    f32, bf16 = jnp.float32, jnp.bfloat16

    top = n_row // 2
    plan = Plan(channels, 2)
    own = (me_row // top).astype(jnp.int32).reshape(1)
    other = 1 - own

    keys = keys.reshape(frames, tokens, channels)
    values = values.reshape(frames, tokens, channels)
    odd = (me_row % 2).astype(jnp.int32).reshape(1)
    send, mine, far, *near = sums(plan, own, odd, keys, values, queries)
    got = swap(send, "row", top)
    far, forward = cross(far)
    near = [swap(edge, "row", 1) for edge in near]
    mine = mine + got.astype(f32)

    total = jnp.sum(mine, axis=0)
    moving = total.astype(bf16)
    neighbour = swap(moving, "frame", 1).astype(f32)
    second = (me_frame % 2) == 1
    before = jnp.where(second, neighbour, 0.0)
    running = total + neighbour
    pairs = n_frame // 2
    reach = 1
    while reach < pairs:
        hop = [(i, i + 2 * reach) for i in range(n_frame - 2 * reach)]
        moving = running.astype(bf16)
        if reach == 2:
            moving, far = lax.optimization_barrier((moving, far))
        earlier = lax.ppermute(moving, "frame", hop).astype(f32)
        before = before + earlier
        running = running + earlier
        reach *= 2
    states = before[None] + jnp.cumsum(mine, axis=0)
    bit = 1
    while bit < top:
        moving = states.astype(bf16)
        if bit == 1:
            moving, near[-1] = lax.optimization_barrier((moving, near[-1]))
            moving, queries, gate = lax.optimization_barrier((moving, queries, gate))
            qf, sg = ready(plan, queries, gate)
        arrived = swap(moving, "row", bit)
        if bit == 1:
            arrived, qf, sg = lax.optimization_barrier((arrived, qf, sg))
        states = states + arrived.astype(f32)
        bit *= 2
    states = states.astype(bf16)
    others = swap(states, "row", top)

    far = forward(far)
    shape = queries.shape
    out = mix(plan, shape, own, odd, states, qf, near, far, sg, conv_weight, None)
    return mix(plan, shape, other, odd, others, qf, near, far, sg, conv_weight, out)


def solution(mesh):
    spec = P("frame", "row", None, None)
    return jax.shard_map(
        per_device,
        mesh=mesh,
        in_specs=(spec, spec, spec, spec, P()),
        out_specs=spec,
        check_vma=False,
    )
```

```python
import functools

import jax
import jax.numpy as jnp
from jax import lax
from jax.experimental import pallas as pl
from jax.experimental.pallas import tpu as pltpu
from jax.sharding import PartitionSpec as P

HEAD_DIM = 32
LANES = 128
GROUP = LANES // HEAD_DIM
Z_ALIGN = 16
MARGIN = 8
CHUNK = 16
PARTS = 2
SUMS_LIMIT = 60 << 20
READY_LIMIT = 52 << 20
MIX_LIMIT = 40 << 20


def ceil_div(a, b):
    return -(-a // b)


class Plan:
    def __init__(self, channels, halves):
        total = ceil_div(channels, LANES)
        self.channels = channels
        self.halves = halves
        self.blocks = ceil_div(total, halves)
        self.per = max(p for p in (1, 2, 3) if self.blocks % p == 0)
        self.steps = self.blocks // self.per
        self.z_row = self.blocks * HEAD_DIM
        self.rows = self.z_row + ceil_div(self.blocks, Z_ALIGN) * Z_ALIGN
        self.width = self.per * LANES


def same_head():
    row = lax.broadcasted_iota(jnp.int32, (LANES, LANES), 0) // HEAD_DIM
    col = lax.broadcasted_iota(jnp.int32, (LANES, LANES), 1) // HEAD_DIM
    return row == col


def sums_kernel(
    plan,
    own_ref,
    odd_ref,
    k_hbm,
    v_hbm,
    q_hbm,
    send_ref,
    mine_ref,
    far_ref,
    *rest,
):
    *near_refs, k_ref, v_ref, acc_ref, sems, edge_sems = rest
    frames, tokens, channels = k_ref.shape
    rows = q_hbm.shape[1]
    part = tokens // PARTS
    odd = odd_ref[0]
    copies = []
    for f in range(frames):
        for p in range(PARTS):
            at = (f, pl.ds(p * part, part))
            copies.append(
                [
                    pltpu.make_async_copy(k_hbm.at[at], k_ref.at[at], sems.at[0, f, p]),
                    pltpu.make_async_copy(v_hbm.at[at], v_ref.at[at], sems.at[1, f, p]),
                ]
            )
    edges = [
        pltpu.make_async_copy(
            q_hbm.at[:, pl.ds((rows - 1) * (1 - odd), 1)], near, edge_sems.at[f]
        )
        for f, near in enumerate(near_refs)
    ]
    edges.append(
        pltpu.make_async_copy(
            q_hbm.at[:, pl.ds((rows - 1) * odd, 1)], far_ref, edge_sems.at[1]
        )
    )
    for pair in copies:
        for copy in pair:
            copy.start()
    for edge in edges:
        edge.start()

    mask = same_head()
    acc_ref[:, :, plan.z_row :, :] = jnp.zeros(
        (plan.halves, frames, plan.rows - plan.z_row, LANES), jnp.float32
    )
    for f in range(frames):
        for pair in copies[f * PARTS : (f + 1) * PARTS]:
            for copy in pair:
                copy.wait()
        for index in range(ceil_div(channels, LANES)):
            half, block = divmod(index, plan.blocks)
            lanes = slice(index * LANES, min((index + 1) * LANES, channels))
            kf = jnp.maximum(k_ref[f, :, lanes], 0)
            v = v_ref[f, :, lanes]
            if kf.shape[1] < LANES:
                rest = jnp.zeros((tokens, LANES - kf.shape[1]), kf.dtype)
                kf = jnp.concatenate([kf, rest], axis=1)
                v = jnp.concatenate([v, rest], axis=1)
            full = lax.dot_general(
                kf, v, (((0,), (0,)), ((), ())), preferred_element_type=jnp.float32
            )
            full = jnp.where(mask, full, 0.0)
            state = full.reshape(GROUP, HEAD_DIM, LANES).sum(axis=0)
            norm = jnp.sum(kf.astype(jnp.float32), axis=0, keepdims=True)
            acc_ref[half, f, block * HEAD_DIM : (block + 1) * HEAD_DIM, :] = state
            acc_ref[half, f, plan.z_row + block : plan.z_row + block + 1, :] = norm
    own = own_ref[0]
    mine_ref[...] = acc_ref[own]
    send_ref[...] = acc_ref[1 - own].astype(send_ref.dtype)
    for edge in edges:
        edge.wait()


def sums(plan, own, odd, keys, values, queries):
    frames, tokens, channels = keys.shape
    _, rows, width, _ = queries.shape
    scalar = pl.BlockSpec(memory_space=pltpu.SMEM)
    anywhere = pl.BlockSpec(memory_space=pl.ANY)
    whole = pl.BlockSpec(memory_space=pltpu.VMEM)
    state = (frames, plan.rows, LANES)
    return pl.pallas_call(
        functools.partial(sums_kernel, plan),
        in_specs=[scalar, scalar, anywhere, anywhere, anywhere],
        out_specs=[whole] * 4,
        scratch_shapes=[
            pltpu.VMEM((frames, tokens, channels), keys.dtype),
            pltpu.VMEM((frames, tokens, channels), values.dtype),
            pltpu.VMEM((plan.halves, frames, plan.rows, LANES), jnp.float32),
            pltpu.SemaphoreType.DMA((2, frames, PARTS)),
            pltpu.SemaphoreType.DMA((2,)),
        ],
        out_shape=[
            pltpu.VMEM(state, jnp.bfloat16),
            pltpu.VMEM(state, jnp.float32),
            pltpu.VMEM((frames, 1, width, channels), queries.dtype),
        ]
        + [pltpu.VMEM((frames, 1, width, channels), queries.dtype)],
        compiler_params=pltpu.CompilerParams(vmem_limit_bytes=SUMS_LIMIT),
        cost_estimate=pl.CostEstimate(
            flops=2 * frames * tokens * channels * LANES,
            bytes_accessed=4 * frames * tokens * channels,
            transcendentals=0,
        ),
        name="sums",
    )(own, odd, keys, values, queries)


def ready_kernel(plan, q_ref, g_ref, qf_ref, sg_ref):
    step = pl.program_id(0)
    frames, tokens = qf_ref.shape[1:3]
    lane = lax.broadcasted_iota(jnp.int32, (1, LANES), 1)
    for b in range(plan.per):
        lanes = slice(b * LANES, (b + 1) * LANES)
        block = step * plan.per + b
        live = lane + block * LANES < plan.channels
        q = q_ref[:, :, :, lanes].reshape(frames, tokens, LANES)
        qf_ref[block] = jnp.where(live, jnp.maximum(q, 0), jnp.zeros_like(q))
        g = 0.5 * g_ref[:, :, :, lanes].astype(jnp.float32).reshape(frames, tokens, LANES)
        sg_ref[block] = g + g * jnp.tanh(g)


def ready(plan, queries, gate):
    frames, rows, width, channels = queries.shape
    body = pl.BlockSpec((frames, rows, width, plan.width), lambda i: (0, 0, 0, i))
    whole = pl.BlockSpec(memory_space=pltpu.VMEM)
    shape = (plan.halves * plan.blocks, frames, rows * width, LANES)
    return pl.pallas_call(
        functools.partial(ready_kernel, plan),
        grid=(plan.halves * plan.steps,),
        in_specs=[body, body],
        out_specs=[whole, whole],
        out_shape=[pltpu.VMEM(shape, jnp.bfloat16), pltpu.VMEM(shape, jnp.float32)],
        compiler_params=pltpu.CompilerParams(
            dimension_semantics=("arbitrary",), vmem_limit_bytes=READY_LIMIT
        ),
        cost_estimate=pl.CostEstimate(
            flops=8 * frames * rows * width * channels,
            bytes_accessed=10 * frames * rows * width * channels,
            transcendentals=frames * rows * width * channels,
        ),
        name="ready",
    )(queries, gate)


def mix_kernel(plan, shape, half_ref, odd_ref, s_ref, qf_ref, sg_ref, w_ref, far_ref, *rest):
    o_ref, att_ref = rest[-2:]
    near_ref = rest[0]
    frames, rows, width = shape
    step = pl.program_id(0)
    ones = same_head().astype(jnp.bfloat16)
    nothing = jnp.zeros_like(ones)
    lower = jnp.concatenate([nothing, ones], axis=1)
    z_iota = lax.broadcasted_iota(jnp.int32, (plan.rows - plan.z_row, LANES), 0)
    lane = lax.broadcasted_iota(jnp.int32, (1, LANES), 1)
    first = (half_ref[0] * plan.steps + step) * plan.width

    half_block = half_ref[0] * plan.blocks
    near_row = (rows + 1) * (1 - odd_ref[0])

    @pl.when(step == 0)
    def _():
        side = jnp.zeros(att_ref.shape[:2] + (MARGIN, LANES), jnp.float32)
        att_ref[:, :, :MARGIN, :] = side
        att_ref[:, :, MARGIN + width :, :] = side

    for f in range(frames):
        zs = s_ref[f, plan.z_row :, :].astype(jnp.float32)
        for b in range(plan.per):
            slot = (f * plan.per + b) % att_ref.shape[0]
            lanes = slice(b * LANES, (b + 1) * LANES)
            block = step * plan.per + b
            live = lane + (first + b * LANES) < plan.channels
            state = s_ref[f, pl.ds(pl.multiple_of(block * HEAD_DIM, HEAD_DIM), HEAD_DIM), :]
            numer = jnp.concatenate([state] * GROUP, axis=0) * ones
            weights = jnp.concatenate(
                [jnp.concatenate([numer, nothing], axis=1), lower], axis=0
            )
            z = jnp.sum(jnp.where(z_iota == block, zs, 0.0), axis=0, keepdims=True)
            z = z.astype(jnp.bfloat16)
            edge = jnp.concatenate(
                [
                    near_ref[f, :, :, lanes].reshape(width, LANES),
                    far_ref[f, :, :, lanes].reshape(width, LANES),
                ],
                axis=0,
            )
            edge = jnp.where(live, jnp.maximum(edge, 0), jnp.zeros_like(edge))
            qf = jnp.concatenate([qf_ref[half_block + block, f], edge], axis=0)
            both = jnp.dot(
                jnp.concatenate([qf, qf * z], axis=1),
                weights,
                preferred_element_type=jnp.float32,
            )
            att = both[:, :LANES] * pltpu.reciprocal(both[:, LANES:] + 1e-6, approx=True)
            att = att.reshape(rows + 2, width, LANES)
            att_ref[slot, 1 : rows + 1, MARGIN : MARGIN + width, :] = att[:rows]
            att_ref[slot, near_row, MARGIN : MARGIN + width, :] = att[rows]
            att_ref[slot, rows + 1 - near_row, MARGIN : MARGIN + width, :] = att[rows + 1]
            taps = [[w_ref[a, c, lanes] for c in range(3)] for a in range(3)]
            for start in range(0, width, CHUNK):
                near = [
                    [
                        att_ref[slot, r, pl.ds(MARGIN - 1 + c + start, CHUNK), :]
                        for c in range(3)
                    ]
                    for r in range(rows + 2)
                ]
                for r in range(rows):
                    conv = None
                    for a in range(3):
                        for c in range(3):
                            term = near[r + a][c] * taps[a][c]
                            conv = term if conv is None else conv + term
                    at = r * width + start
                    mixed = conv * sg_ref[half_block + block, f, at : at + CHUNK, :]
                    o_ref[f, r, start : start + CHUNK, lanes] = mixed.astype(o_ref.dtype)


def mix(plan, shape, half, odd, states, qf, near, far, sg, weight, earlier):
    frames, rows, width, channels = shape
    col = lambda i, half, odd: (0, 0, 0, half[0] * plan.steps + i)
    body = pl.BlockSpec((frames, rows, width, plan.width), col)
    edge = lambda n: pl.BlockSpec((n, 1, width, plan.width), col)
    whole = pl.BlockSpec(memory_space=pltpu.VMEM)
    in_specs = [
        whole,
        whole,
        whole,
        pl.BlockSpec((3, 3, plan.width), lambda i, half, odd: (0, 0, half[0] * plan.steps + i)),
        edge(frames),
        edge(frames),
    ]
    operands = [states, qf, sg, weight, far, *near]
    aliases = {}
    if earlier is not None:
        in_specs.append(pl.BlockSpec(memory_space=pl.ANY))
        operands.append(earlier)
        aliases = {8: 0}
    tokens = frames * (rows + 2) * width
    return pl.pallas_call(
        functools.partial(mix_kernel, plan, (frames, rows, width)),
        grid_spec=pltpu.PrefetchScalarGridSpec(
            num_scalar_prefetch=2,
            grid=(plan.steps,),
            in_specs=in_specs,
            out_specs=body,
            scratch_shapes=[
                pltpu.VMEM((2, rows + 2, width + 2 * MARGIN, LANES), jnp.float32)
            ],
        ),
        out_shape=jax.ShapeDtypeStruct(shape, jnp.bfloat16),
        input_output_aliases=aliases,
        compiler_params=pltpu.CompilerParams(
            dimension_semantics=("arbitrary",), vmem_limit_bytes=MIX_LIMIT
        ),
        cost_estimate=pl.CostEstimate(
            flops=2 * tokens * plan.blocks * LANES * LANES * 2,
            bytes_accessed=8 * tokens * plan.blocks * LANES,
            transcendentals=tokens * plan.blocks * LANES,
        ),
        name="mix",
    )(half, odd, *operands)


def swap(array, axis, bit):
    n = lax.axis_size(axis)
    return lax.ppermute(array, axis, [(i, i ^ bit) for i in range(n)])


def cross(edge):
    n_row, n_frame = lax.axis_size("row"), lax.axis_size("frame")
    pairs = [(i, i + 1) for i in range(1, n_row - 1, 2)]
    pairs = pairs + [(j, i) for i, j in pairs]
    if n_row != 4 or n_frame % 2:
        return lax.ppermute(edge, "row", pairs), lambda held: held
    both = ("frame", "row")
    one, two = [], []
    for f in range(n_frame):
        for i, j in pairs:
            corner = i ^ 2
            if f % 2:
                one.append((f * n_row + i, f * n_row + corner))
                two.append((f * n_row + corner, f * n_row + j))
            else:
                one.append((f * n_row + i, f * n_row + j))
                two.append((f * n_row + j, f * n_row + j))
    return lax.ppermute(edge, both, one), lambda held: lax.ppermute(held, both, two)


def per_device(queries, keys, values, gate, conv_weight):
    frames, rows, width, channels = queries.shape
    tokens = rows * width
    n_row, n_frame = lax.axis_size("row"), lax.axis_size("frame")
    me_row, me_frame = lax.axis_index("row"), lax.axis_index("frame")
    f32, bf16 = jnp.float32, jnp.bfloat16

    top = n_row // 2
    plan = Plan(channels, 2)
    own = (me_row // top).astype(jnp.int32).reshape(1)
    other = 1 - own

    keys = keys.reshape(frames, tokens, channels)
    values = values.reshape(frames, tokens, channels)
    odd = (me_row % 2).astype(jnp.int32).reshape(1)
    send, mine, far, *near = sums(plan, own, odd, keys, values, queries)
    got = swap(send, "row", top)
    far, forward = cross(far)
    near = [swap(edge, "row", 1) for edge in near]
    mine = mine + got.astype(f32)

    second = (me_frame % 2) == 1
    reaches = [1 << i for i in range((n_frame // 2 - 1).bit_length())]
    once = jnp.minimum(me_frame + 1, 1)

    def arriving(running, reach):
        hop = [(i, i + 2 * reach) for i in range(n_frame - 2 * reach)]
        return lax.ppermute(running.astype(bf16), "frame", hop).astype(f32)

    def nearest(_, carry):
        _, total = carry
        neighbour = swap(total.astype(bf16), "frame", 1).astype(f32)
        before, running = jnp.where(second, neighbour, 0.0), total + neighbour
        for reach in reaches[:1]:
            earlier = arriving(running, reach)
            before, running = before + earlier, running + earlier
        return before, running

    def farther(_, before):
        ahead = running
        for reach in reaches[1:]:
            earlier = arriving(ahead, reach)
            before, ahead = before + earlier, ahead + earlier
        return before

    total = jnp.sum(mine, axis=0)
    before, running = lax.fori_loop(0, once, nearest, (total, total))
    running, far = lax.optimization_barrier((running, far))
    far = forward(far)
    before = farther(0, before)
    states = before[None] + jnp.cumsum(mine, axis=0)
    bit = 1
    while bit < top:
        moving = states.astype(bf16)
        if bit == 1:
            moving, near[-1] = lax.optimization_barrier((moving, near[-1]))
            moving, queries, gate = lax.optimization_barrier((moving, queries, gate))
            qf, sg = ready(plan, queries, gate)
        arrived = swap(moving, "row", bit)
        if bit == 1:
            arrived, qf, sg = lax.optimization_barrier((arrived, qf, sg))
        states = states + arrived.astype(f32)
        bit *= 2
    states = states.astype(bf16)
    others = swap(states, "row", top)

    shape = queries.shape
    out = mix(plan, shape, own, odd, states, qf, near, far, sg, conv_weight, None)
    return mix(plan, shape, other, odd, others, qf, near, far, sg, conv_weight, out)


def solution(mesh):
    spec = P("frame", "row", None, None)
    return jax.shard_map(
        per_device,
        mesh=mesh,
        in_specs=(spec, spec, spec, spec, P()),
        out_specs=spec,
        check_vma=False,
    )
```

```python
import functools

import jax
import jax.numpy as jnp
from jax import lax
from jax.experimental import pallas as pl
from jax.experimental.pallas import tpu as pltpu
from jax.sharding import PartitionSpec as P

HEAD_DIM = 32
LANES = 128
GROUP = LANES // HEAD_DIM
Z_ALIGN = 16
MARGIN = 8
CHUNK = 16
PARTS = 2
SUMS_LIMIT = 60 << 20
READY_LIMIT = 52 << 20
MIX_LIMIT = 40 << 20


def ceil_div(a, b):
    return -(-a // b)


class Plan:
    def __init__(self, channels, halves):
        total = ceil_div(channels, LANES)
        self.channels = channels
        self.halves = halves
        self.blocks = ceil_div(total, halves)
        self.per = max(p for p in (1, 2, 3) if self.blocks % p == 0)
        self.steps = self.blocks // self.per
        self.z_row = self.blocks * HEAD_DIM
        self.rows = self.z_row + ceil_div(self.blocks, Z_ALIGN) * Z_ALIGN
        self.width = self.per * LANES


def same_head():
    row = lax.broadcasted_iota(jnp.int32, (LANES, LANES), 0) // HEAD_DIM
    col = lax.broadcasted_iota(jnp.int32, (LANES, LANES), 1) // HEAD_DIM
    return row == col


def sums_kernel(
    plan,
    own_ref,
    odd_ref,
    k_hbm,
    v_hbm,
    q_hbm,
    send_ref,
    mine_ref,
    far_ref,
    *rest,
):
    *near_refs, k_ref, v_ref, acc_ref, sems, edge_sems = rest
    frames, tokens, channels = k_ref.shape
    rows = q_hbm.shape[1]
    part = tokens // PARTS
    odd = odd_ref[0]
    copies = []
    for f in range(frames):
        for p in range(PARTS):
            at = (f, pl.ds(p * part, part))
            copies.append(
                [
                    pltpu.make_async_copy(k_hbm.at[at], k_ref.at[at], sems.at[0, f, p]),
                    pltpu.make_async_copy(v_hbm.at[at], v_ref.at[at], sems.at[1, f, p]),
                ]
            )
    edges = [
        pltpu.make_async_copy(
            q_hbm.at[:, pl.ds((rows - 1) * (1 - odd), 1)], near, edge_sems.at[f]
        )
        for f, near in enumerate(near_refs)
    ]
    edges.append(
        pltpu.make_async_copy(
            q_hbm.at[:, pl.ds((rows - 1) * odd, 1)], far_ref, edge_sems.at[1]
        )
    )
    for pair in copies:
        for copy in pair:
            copy.start()
    for edge in edges:
        edge.start()

    mask = same_head()
    acc_ref[:, :, plan.z_row :, :] = jnp.zeros(
        (plan.halves, frames, plan.rows - plan.z_row, LANES), jnp.float32
    )
    for f in range(frames):
        for pair in copies[f * PARTS : (f + 1) * PARTS]:
            for copy in pair:
                copy.wait()
        for index in range(ceil_div(channels, LANES)):
            half, block = divmod(index, plan.blocks)
            lanes = slice(index * LANES, min((index + 1) * LANES, channels))
            kf = jnp.maximum(k_ref[f, :, lanes], 0)
            v = v_ref[f, :, lanes]
            if kf.shape[1] < LANES:
                rest = jnp.zeros((tokens, LANES - kf.shape[1]), kf.dtype)
                kf = jnp.concatenate([kf, rest], axis=1)
                v = jnp.concatenate([v, rest], axis=1)
            full = lax.dot_general(
                kf, v, (((0,), (0,)), ((), ())), preferred_element_type=jnp.float32
            )
            full = jnp.where(mask, full, 0.0)
            state = full.reshape(GROUP, HEAD_DIM, LANES).sum(axis=0)
            norm = jnp.sum(kf.astype(jnp.float32), axis=0, keepdims=True)
            acc_ref[half, f, block * HEAD_DIM : (block + 1) * HEAD_DIM, :] = state
            acc_ref[half, f, plan.z_row + block : plan.z_row + block + 1, :] = norm
    own = own_ref[0]
    mine_ref[...] = acc_ref[own]
    send_ref[...] = acc_ref[1 - own].astype(send_ref.dtype)
    for edge in edges:
        edge.wait()


def sums(plan, own, odd, keys, values, queries):
    frames, tokens, channels = keys.shape
    _, rows, width, _ = queries.shape
    scalar = pl.BlockSpec(memory_space=pltpu.SMEM)
    anywhere = pl.BlockSpec(memory_space=pl.ANY)
    whole = pl.BlockSpec(memory_space=pltpu.VMEM)
    state = (frames, plan.rows, LANES)
    return pl.pallas_call(
        functools.partial(sums_kernel, plan),
        in_specs=[scalar, scalar, anywhere, anywhere, anywhere],
        out_specs=[whole] * 4,
        scratch_shapes=[
            pltpu.VMEM((frames, tokens, channels), keys.dtype),
            pltpu.VMEM((frames, tokens, channels), values.dtype),
            pltpu.VMEM((plan.halves, frames, plan.rows, LANES), jnp.float32),
            pltpu.SemaphoreType.DMA((2, frames, PARTS)),
            pltpu.SemaphoreType.DMA((2,)),
        ],
        out_shape=[
            pltpu.VMEM(state, jnp.bfloat16),
            pltpu.VMEM(state, jnp.float32),
            pltpu.VMEM((frames, 1, width, channels), queries.dtype),
        ]
        + [pltpu.VMEM((frames, 1, width, channels), queries.dtype)],
        compiler_params=pltpu.CompilerParams(vmem_limit_bytes=SUMS_LIMIT),
        cost_estimate=pl.CostEstimate(
            flops=2 * frames * tokens * channels * LANES,
            bytes_accessed=4 * frames * tokens * channels,
            transcendentals=0,
        ),
        name="sums",
    )(own, odd, keys, values, queries)


def ready_kernel(plan, q_ref, g_ref, qf_ref, sg_ref):
    step = pl.program_id(0)
    frames, tokens = qf_ref.shape[1:3]
    lane = lax.broadcasted_iota(jnp.int32, (1, LANES), 1)
    for b in range(plan.blocks):
        lanes = slice(b * LANES, (b + 1) * LANES)
        block = step * plan.blocks + b
        live = lane + block * LANES < plan.channels
        q = q_ref[:, :, :, lanes].reshape(frames, tokens, LANES)
        qf_ref[block] = jnp.where(live, jnp.maximum(q, 0), jnp.zeros_like(q))
        g = 0.5 * g_ref[:, :, :, lanes].astype(jnp.float32).reshape(frames, tokens, LANES)
        sg_ref[block] = g + g * jnp.tanh(g)


def ready(plan, queries, gate):
    frames, rows, width, channels = queries.shape
    body = pl.BlockSpec((frames, rows, width, plan.blocks * LANES), lambda i: (0, 0, 0, i))
    whole = pl.BlockSpec(memory_space=pltpu.VMEM)
    shape = (plan.halves * plan.blocks, frames, rows * width, LANES)
    return pl.pallas_call(
        functools.partial(ready_kernel, plan),
        grid=(plan.halves,),
        in_specs=[body, body],
        out_specs=[whole, whole],
        out_shape=[pltpu.VMEM(shape, jnp.bfloat16), pltpu.VMEM(shape, jnp.float32)],
        compiler_params=pltpu.CompilerParams(
            dimension_semantics=("arbitrary",), vmem_limit_bytes=READY_LIMIT
        ),
        cost_estimate=pl.CostEstimate(
            flops=8 * frames * rows * width * channels,
            bytes_accessed=10 * frames * rows * width * channels,
            transcendentals=frames * rows * width * channels,
        ),
        name="ready",
    )(queries, gate)


def mix_kernel(plan, shape, half_ref, odd_ref, s_ref, qf_ref, sg_ref, w_ref, far_ref, *rest):
    o_ref, att_ref = rest[-2:]
    near_ref = rest[0]
    frames, rows, width = shape
    step = pl.program_id(0)
    ones = same_head().astype(jnp.bfloat16)
    nothing = jnp.zeros_like(ones)
    lower = jnp.concatenate([nothing, ones], axis=1)
    z_iota = lax.broadcasted_iota(jnp.int32, (plan.rows - plan.z_row, LANES), 0)
    lane = lax.broadcasted_iota(jnp.int32, (1, LANES), 1)
    first = (half_ref[0] * plan.steps + step) * plan.width

    half_block = half_ref[0] * plan.blocks
    near_row = (rows + 1) * (1 - odd_ref[0])

    @pl.when(step == 0)
    def _():
        side = jnp.zeros(att_ref.shape[:2] + (MARGIN, LANES), jnp.float32)
        att_ref[:, :, :MARGIN, :] = side
        att_ref[:, :, MARGIN + width :, :] = side

    for f in range(frames):
        zs = s_ref[f, plan.z_row :, :].astype(jnp.float32)
        for b in range(plan.per):
            slot = (f * plan.per + b) % att_ref.shape[0]
            lanes = slice(b * LANES, (b + 1) * LANES)
            block = step * plan.per + b
            live = lane + (first + b * LANES) < plan.channels
            state = s_ref[f, pl.ds(pl.multiple_of(block * HEAD_DIM, HEAD_DIM), HEAD_DIM), :]
            numer = jnp.concatenate([state] * GROUP, axis=0) * ones
            weights = jnp.concatenate(
                [jnp.concatenate([numer, nothing], axis=1), lower], axis=0
            )
            z = jnp.sum(jnp.where(z_iota == block, zs, 0.0), axis=0, keepdims=True)
            z = z.astype(jnp.bfloat16)
            edge = jnp.concatenate(
                [
                    near_ref[f, :, :, lanes].reshape(width, LANES),
                    far_ref[f, :, :, lanes].reshape(width, LANES),
                ],
                axis=0,
            )
            edge = jnp.where(live, jnp.maximum(edge, 0), jnp.zeros_like(edge))
            qf = jnp.concatenate([qf_ref[half_block + block, f], edge], axis=0)
            both = jnp.dot(
                jnp.concatenate([qf, qf * z], axis=1),
                weights,
                preferred_element_type=jnp.float32,
            )
            att = both[:, :LANES] * pltpu.reciprocal(both[:, LANES:] + 1e-6, approx=True)
            att = att.reshape(rows + 2, width, LANES)
            att_ref[slot, 1 : rows + 1, MARGIN : MARGIN + width, :] = att[:rows]
            att_ref[slot, near_row, MARGIN : MARGIN + width, :] = att[rows]
            att_ref[slot, rows + 1 - near_row, MARGIN : MARGIN + width, :] = att[rows + 1]
            taps = [[w_ref[a, c, lanes] for c in range(3)] for a in range(3)]
            for start in range(0, width, CHUNK):
                near = [
                    [
                        att_ref[slot, r, pl.ds(MARGIN - 1 + c + start, CHUNK), :]
                        for c in range(3)
                    ]
                    for r in range(rows + 2)
                ]
                for r in range(rows):
                    conv = None
                    for a in range(3):
                        for c in range(3):
                            term = near[r + a][c] * taps[a][c]
                            conv = term if conv is None else conv + term
                    at = r * width + start
                    mixed = conv * sg_ref[half_block + block, f, at : at + CHUNK, :]
                    o_ref[f, r, start : start + CHUNK, lanes] = mixed.astype(o_ref.dtype)


def mix(plan, shape, half, odd, states, qf, near, far, sg, weight, earlier):
    frames, rows, width, channels = shape
    col = lambda i, half, odd: (0, 0, 0, half[0] * plan.steps + i)
    body = pl.BlockSpec((frames, rows, width, plan.width), col)
    edge = lambda n: pl.BlockSpec((n, 1, width, plan.width), col)
    whole = pl.BlockSpec(memory_space=pltpu.VMEM)
    in_specs = [
        whole,
        whole,
        whole,
        pl.BlockSpec((3, 3, plan.width), lambda i, half, odd: (0, 0, half[0] * plan.steps + i)),
        edge(frames),
        edge(frames),
    ]
    operands = [states, qf, sg, weight, far, *near]
    aliases = {}
    if earlier is not None:
        in_specs.append(pl.BlockSpec(memory_space=pl.ANY))
        operands.append(earlier)
        aliases = {8: 0}
    tokens = frames * (rows + 2) * width
    return pl.pallas_call(
        functools.partial(mix_kernel, plan, (frames, rows, width)),
        grid_spec=pltpu.PrefetchScalarGridSpec(
            num_scalar_prefetch=2,
            grid=(plan.steps,),
            in_specs=in_specs,
            out_specs=body,
            scratch_shapes=[
                pltpu.VMEM((1, rows + 2, width + 2 * MARGIN, LANES), jnp.float32)
            ],
        ),
        out_shape=jax.ShapeDtypeStruct(shape, jnp.bfloat16),
        input_output_aliases=aliases,
        compiler_params=pltpu.CompilerParams(
            dimension_semantics=("arbitrary",), vmem_limit_bytes=MIX_LIMIT
        ),
        cost_estimate=pl.CostEstimate(
            flops=2 * tokens * plan.blocks * LANES * LANES * 2,
            bytes_accessed=8 * tokens * plan.blocks * LANES,
            transcendentals=tokens * plan.blocks * LANES,
        ),
        name="mix",
    )(half, odd, *operands)


def swap(array, axis, bit):
    n = lax.axis_size(axis)
    return lax.ppermute(array, axis, [(i, i ^ bit) for i in range(n)])


def cross(edge):
    n_row, n_frame = lax.axis_size("row"), lax.axis_size("frame")
    pairs = [(i, i + 1) for i in range(1, n_row - 1, 2)]
    pairs = pairs + [(j, i) for i, j in pairs]
    if n_row != 4 or n_frame % 2:
        return edge, lambda held: lax.ppermute(held, "row", pairs)
    both = ("frame", "row")
    one, two = [], []
    for f in range(n_frame):
        for i, j in pairs:
            via = i ^ 2 if f % 2 else i
            one.append((f * n_row + i, f * n_row + via))
            two.append((f * n_row + via, f * n_row + j))
    return lax.ppermute(edge, both, one), lambda held: lax.ppermute(held, both, two)


def per_device(queries, keys, values, gate, conv_weight):
    frames, rows, width, channels = queries.shape
    tokens = rows * width
    n_row, n_frame = lax.axis_size("row"), lax.axis_size("frame")
    me_row, me_frame = lax.axis_index("row"), lax.axis_index("frame")
    f32, bf16 = jnp.float32, jnp.bfloat16

    top = n_row // 2
    plan = Plan(channels, 2)
    own = (me_row // top).astype(jnp.int32).reshape(1)
    other = 1 - own

    keys = keys.reshape(frames, tokens, channels)
    values = values.reshape(frames, tokens, channels)
    odd = (me_row % 2).astype(jnp.int32).reshape(1)
    send, mine, far, *near = sums(plan, own, odd, keys, values, queries)
    got = swap(send, "row", top)
    far, forward = cross(far)
    near = [swap(edge, "row", 1) for edge in near]
    mine = mine + got.astype(f32)

    second = (me_frame % 2) == 1
    reaches = [1 << i for i in range((n_frame // 2 - 1).bit_length())]
    once = jnp.minimum(me_frame + 1, 1)

    def arriving(running, reach):
        hop = [(i, i + 2 * reach) for i in range(n_frame - 2 * reach)]
        return lax.ppermute(running, "frame", hop)

    def nearest(_, carry):
        total, moving = carry
        neighbour = swap(moving, "frame", 1).astype(f32)
        before, running = jnp.where(second, neighbour, 0.0), (total + neighbour).astype(bf16)
        for reach in reaches[:1]:
            earlier = arriving(running, reach).astype(f32)
            before, running = before + earlier, (total + neighbour + earlier).astype(bf16)
        return before, running

    def farther(_, carry):
        before, running = carry
        for reach in reaches[1:]:
            earlier = arriving(running, reach)
            before = before + earlier.astype(f32)
            running = (running.astype(f32) + earlier.astype(f32)).astype(bf16)
        return before, running

    total = jnp.sum(mine, axis=0)
    before, running = lax.fori_loop(0, once, nearest, (total, total.astype(bf16)))
    running, far = lax.optimization_barrier((running, far))
    far = forward(far)
    before, _ = lax.fori_loop(0, once, farther, (before, running))
    states = before[None] + jnp.cumsum(mine, axis=0)
    bit = 1
    while bit < top:
        moving = states.astype(bf16)
        if bit == 1:
            moving, near[-1] = lax.optimization_barrier((moving, near[-1]))
            moving, queries, gate = lax.optimization_barrier((moving, queries, gate))
            qf, sg = ready(plan, queries, gate)
        arrived = swap(moving, "row", bit)
        if bit == 1:
            arrived, qf, sg = lax.optimization_barrier((arrived, qf, sg))
        states = states + arrived.astype(f32)
        bit *= 2
    states = states.astype(bf16)
    others = swap(states, "row", top)

    shape = queries.shape
    out = mix(plan, shape, own, odd, states, qf, near, far, sg, conv_weight, None)
    return mix(plan, shape, other, odd, others, qf, near, far, sg, conv_weight, out)


def solution(mesh):
    spec = P("frame", "row", None, None)
    return jax.shard_map(
        per_device,
        mesh=mesh,
        in_specs=(spec, spec, spec, spec, P()),
        out_specs=spec,
        check_vma=False,
    )
```

```python
import functools

import jax
import jax.numpy as jnp
from jax import lax
from jax.experimental import pallas as pl
from jax.experimental.pallas import tpu as pltpu
from jax.sharding import PartitionSpec as P

HEAD_DIM = 32
LANES = 128
GROUP = LANES // HEAD_DIM
Z_ALIGN = 16
MARGIN = 8
CHUNK = 16
PARTS = 2
SUMS_LIMIT = 60 << 20
READY_LIMIT = 52 << 20
MIX_LIMIT = 40 << 20


def ceil_div(a, b):
    return -(-a // b)


class Plan:
    def __init__(self, channels, halves):
        total = ceil_div(channels, LANES)
        self.channels = channels
        self.halves = halves
        self.blocks = ceil_div(total, halves)
        self.per = max(p for p in (1, 2, 3) if self.blocks % p == 0)
        self.steps = self.blocks // self.per
        self.z_row = self.blocks * HEAD_DIM
        self.rows = self.z_row + ceil_div(self.blocks, Z_ALIGN) * Z_ALIGN
        self.width = self.per * LANES


def same_head():
    row = lax.broadcasted_iota(jnp.int32, (LANES, LANES), 0) // HEAD_DIM
    col = lax.broadcasted_iota(jnp.int32, (LANES, LANES), 1) // HEAD_DIM
    return row == col


def sums_kernel(
    plan,
    own_ref,
    odd_ref,
    k_hbm,
    v_hbm,
    q_hbm,
    send_ref,
    mine_ref,
    far_ref,
    *rest,
):
    *near_refs, k_ref, v_ref, acc_ref, sems, edge_sems = rest
    frames, tokens, channels = k_ref.shape
    rows = q_hbm.shape[1]
    part = tokens // PARTS
    odd = odd_ref[0]
    copies = []
    for f in range(frames):
        for p in range(PARTS):
            at = (f, pl.ds(p * part, part))
            copies.append(
                [
                    pltpu.make_async_copy(k_hbm.at[at], k_ref.at[at], sems.at[0, f, p]),
                    pltpu.make_async_copy(v_hbm.at[at], v_ref.at[at], sems.at[1, f, p]),
                ]
            )
    edges = [
        pltpu.make_async_copy(
            q_hbm.at[:, pl.ds((rows - 1) * (1 - odd), 1)], near, edge_sems.at[f]
        )
        for f, near in enumerate(near_refs)
    ]
    edges.append(
        pltpu.make_async_copy(
            q_hbm.at[:, pl.ds((rows - 1) * odd, 1)], far_ref, edge_sems.at[1]
        )
    )
    for pair in copies:
        for copy in pair:
            copy.start()
    for edge in edges:
        edge.start()

    mask = same_head()
    acc_ref[:, :, plan.z_row :, :] = jnp.zeros(
        (plan.halves, frames, plan.rows - plan.z_row, LANES), jnp.float32
    )
    for f in range(frames):
        for pair in copies[f * PARTS : (f + 1) * PARTS]:
            for copy in pair:
                copy.wait()
        for index in range(ceil_div(channels, LANES)):
            half, block = divmod(index, plan.blocks)
            lanes = slice(index * LANES, min((index + 1) * LANES, channels))
            kf = jnp.maximum(k_ref[f, :, lanes], 0)
            v = v_ref[f, :, lanes]
            if kf.shape[1] < LANES:
                rest = jnp.zeros((tokens, LANES - kf.shape[1]), kf.dtype)
                kf = jnp.concatenate([kf, rest], axis=1)
                v = jnp.concatenate([v, rest], axis=1)
            full = lax.dot_general(
                kf, v, (((0,), (0,)), ((), ())), preferred_element_type=jnp.float32
            )
            full = jnp.where(mask, full, 0.0)
            state = full.reshape(GROUP, HEAD_DIM, LANES).sum(axis=0)
            norm = jnp.sum(kf.astype(jnp.float32), axis=0, keepdims=True)
            acc_ref[half, f, block * HEAD_DIM : (block + 1) * HEAD_DIM, :] = state
            acc_ref[half, f, plan.z_row + block : plan.z_row + block + 1, :] = norm
    own = own_ref[0]
    mine_ref[...] = acc_ref[own]
    send_ref[...] = acc_ref[1 - own].astype(send_ref.dtype)
    for edge in edges:
        edge.wait()


def sums(plan, own, odd, keys, values, queries):
    frames, tokens, channels = keys.shape
    _, rows, width, _ = queries.shape
    scalar = pl.BlockSpec(memory_space=pltpu.SMEM)
    anywhere = pl.BlockSpec(memory_space=pl.ANY)
    whole = pl.BlockSpec(memory_space=pltpu.VMEM)
    state = (frames, plan.rows, LANES)
    return pl.pallas_call(
        functools.partial(sums_kernel, plan),
        in_specs=[scalar, scalar, anywhere, anywhere, anywhere],
        out_specs=[whole] * 4,
        scratch_shapes=[
            pltpu.VMEM((frames, tokens, channels), keys.dtype),
            pltpu.VMEM((frames, tokens, channels), values.dtype),
            pltpu.VMEM((plan.halves, frames, plan.rows, LANES), jnp.float32),
            pltpu.SemaphoreType.DMA((2, frames, PARTS)),
            pltpu.SemaphoreType.DMA((2,)),
        ],
        out_shape=[
            pltpu.VMEM(state, jnp.bfloat16),
            pltpu.VMEM(state, jnp.float32),
            pltpu.VMEM((frames, 1, width, channels), queries.dtype),
        ]
        + [pltpu.VMEM((frames, 1, width, channels), queries.dtype)],
        compiler_params=pltpu.CompilerParams(vmem_limit_bytes=SUMS_LIMIT),
        cost_estimate=pl.CostEstimate(
            flops=2 * frames * tokens * channels * LANES,
            bytes_accessed=4 * frames * tokens * channels,
            transcendentals=0,
        ),
        name="sums",
    )(own, odd, keys, values, queries)


def ready_kernel(plan, q_ref, g_ref, qf_ref, sg_ref):
    step = pl.program_id(0)
    frames, tokens = qf_ref.shape[1:3]
    lane = lax.broadcasted_iota(jnp.int32, (1, LANES), 1)
    for b in range(plan.blocks):
        lanes = slice(b * LANES, (b + 1) * LANES)
        block = step * plan.blocks + b
        live = lane + block * LANES < plan.channels
        q = q_ref[:, :, :, lanes].reshape(frames, tokens, LANES)
        qf_ref[block] = jnp.where(live, jnp.maximum(q, 0), jnp.zeros_like(q))
        g = 0.5 * g_ref[:, :, :, lanes].astype(jnp.float32).reshape(frames, tokens, LANES)
        sg_ref[block] = g + g * jnp.tanh(g)


def ready(plan, queries, gate):
    frames, rows, width, channels = queries.shape
    body = pl.BlockSpec((frames, rows, width, plan.blocks * LANES), lambda i: (0, 0, 0, i))
    whole = pl.BlockSpec(memory_space=pltpu.VMEM)
    shape = (plan.halves * plan.blocks, frames, rows * width, LANES)
    return pl.pallas_call(
        functools.partial(ready_kernel, plan),
        grid=(plan.halves,),
        in_specs=[body, body],
        out_specs=[whole, whole],
        out_shape=[pltpu.VMEM(shape, jnp.bfloat16), pltpu.VMEM(shape, jnp.float32)],
        compiler_params=pltpu.CompilerParams(
            dimension_semantics=("arbitrary",), vmem_limit_bytes=READY_LIMIT
        ),
        cost_estimate=pl.CostEstimate(
            flops=8 * frames * rows * width * channels,
            bytes_accessed=10 * frames * rows * width * channels,
            transcendentals=frames * rows * width * channels,
        ),
        name="ready",
    )(queries, gate)


def mix_kernel(plan, shape, half_ref, odd_ref, s_ref, qf_ref, sg_ref, w_ref, far_ref, *rest):
    o_ref, att_ref = rest[-2:]
    near_ref = rest[0]
    frames, rows, width = shape
    step = pl.program_id(0)
    ones = same_head().astype(jnp.bfloat16)
    nothing = jnp.zeros_like(ones)
    lower = jnp.concatenate([nothing, ones], axis=1)
    z_iota = lax.broadcasted_iota(jnp.int32, (plan.rows - plan.z_row, LANES), 0)
    lane = lax.broadcasted_iota(jnp.int32, (1, LANES), 1)
    first = (half_ref[0] * plan.steps + step) * plan.width

    half_block = half_ref[0] * plan.blocks
    near_row = (rows + 1) * (1 - odd_ref[0])

    @pl.when(step == 0)
    def _():
        side = jnp.zeros(att_ref.shape[:2] + (MARGIN, LANES), jnp.float32)
        att_ref[:, :, :MARGIN, :] = side
        att_ref[:, :, MARGIN + width :, :] = side

    for f in range(frames):
        zs = s_ref[f, plan.z_row :, :].astype(jnp.float32)
        for b in range(plan.per):
            slot = (f * plan.per + b) % att_ref.shape[0]
            lanes = slice(b * LANES, (b + 1) * LANES)
            block = step * plan.per + b
            live = lane + (first + b * LANES) < plan.channels
            state = s_ref[f, pl.ds(pl.multiple_of(block * HEAD_DIM, HEAD_DIM), HEAD_DIM), :]
            numer = jnp.concatenate([state] * GROUP, axis=0) * ones
            weights = jnp.concatenate(
                [jnp.concatenate([numer, nothing], axis=1), lower], axis=0
            )
            z = jnp.sum(jnp.where(z_iota == block, zs, 0.0), axis=0, keepdims=True)
            z = z.astype(jnp.bfloat16)
            edge = jnp.concatenate(
                [
                    near_ref[f, :, :, lanes].reshape(width, LANES),
                    far_ref[f, :, :, lanes].reshape(width, LANES),
                ],
                axis=0,
            )
            edge = jnp.where(live, jnp.maximum(edge, 0), jnp.zeros_like(edge))
            qf = jnp.concatenate([qf_ref[half_block + block, f], edge], axis=0)
            both = jnp.dot(
                jnp.concatenate([qf, qf * z], axis=1),
                weights,
                preferred_element_type=jnp.float32,
            )
            att = both[:, :LANES] * pltpu.reciprocal(both[:, LANES:] + 1e-6, approx=True)
            att = att.reshape(rows + 2, width, LANES)
            att_ref[slot, 1 : rows + 1, MARGIN : MARGIN + width, :] = att[:rows]
            att_ref[slot, near_row, MARGIN : MARGIN + width, :] = att[rows]
            att_ref[slot, rows + 1 - near_row, MARGIN : MARGIN + width, :] = att[rows + 1]
            taps = [[w_ref[a, c, lanes] for c in range(3)] for a in range(3)]
            for start in range(0, width, CHUNK):
                near = [
                    [
                        att_ref[slot, r, pl.ds(MARGIN - 1 + c + start, CHUNK), :]
                        for c in range(3)
                    ]
                    for r in range(rows + 2)
                ]
                for r in range(rows):
                    conv = None
                    for a in range(3):
                        for c in range(3):
                            term = near[r + a][c] * taps[a][c]
                            conv = term if conv is None else conv + term
                    at = r * width + start
                    mixed = conv * sg_ref[half_block + block, f, at : at + CHUNK, :]
                    o_ref[f, r, start : start + CHUNK, lanes] = mixed.astype(o_ref.dtype)


def mix(plan, shape, half, odd, states, qf, near, far, sg, weight, earlier):
    frames, rows, width, channels = shape
    col = lambda i, half, odd: (0, 0, 0, half[0] * plan.steps + i)
    body = pl.BlockSpec((frames, rows, width, plan.width), col)
    edge = lambda n: pl.BlockSpec((n, 1, width, plan.width), col)
    whole = pl.BlockSpec(memory_space=pltpu.VMEM)
    in_specs = [
        whole,
        whole,
        whole,
        pl.BlockSpec((3, 3, plan.width), lambda i, half, odd: (0, 0, half[0] * plan.steps + i)),
        edge(frames),
        edge(frames),
    ]
    operands = [states, qf, sg, weight, far, *near]
    aliases = {}
    if earlier is not None:
        in_specs.append(pl.BlockSpec(memory_space=pl.ANY))
        operands.append(earlier)
        aliases = {8: 0}
    tokens = frames * (rows + 2) * width
    return pl.pallas_call(
        functools.partial(mix_kernel, plan, (frames, rows, width)),
        grid_spec=pltpu.PrefetchScalarGridSpec(
            num_scalar_prefetch=2,
            grid=(plan.steps,),
            in_specs=in_specs,
            out_specs=body,
            scratch_shapes=[
                pltpu.VMEM((1, rows + 2, width + 2 * MARGIN, LANES), jnp.float32)
            ],
        ),
        out_shape=jax.ShapeDtypeStruct(shape, jnp.bfloat16),
        input_output_aliases=aliases,
        compiler_params=pltpu.CompilerParams(
            dimension_semantics=("arbitrary",), vmem_limit_bytes=MIX_LIMIT
        ),
        cost_estimate=pl.CostEstimate(
            flops=2 * tokens * plan.blocks * LANES * LANES * 2,
            bytes_accessed=8 * tokens * plan.blocks * LANES,
            transcendentals=tokens * plan.blocks * LANES,
        ),
        name="mix",
    )(half, odd, *operands)


def swap(array, axis, bit):
    n = lax.axis_size(axis)
    return lax.ppermute(array, axis, [(i, i ^ bit) for i in range(n)])


def cross(edge):
    n_row, n_frame = lax.axis_size("row"), lax.axis_size("frame")
    pairs = [(i, i + 1) for i in range(1, n_row - 1, 2)]
    pairs = pairs + [(j, i) for i, j in pairs]
    if n_row != 4 or n_frame % 2:
        return edge, lambda held: lax.ppermute(held, "row", pairs)
    both = ("frame", "row")
    one, two = [], []
    for f in range(n_frame):
        for i, j in pairs:
            via = i ^ 2 if f % 2 else i
            one.append((f * n_row + i, f * n_row + via))
            two.append((f * n_row + via, f * n_row + j))
    return lax.ppermute(edge, both, one), lambda held: lax.ppermute(held, both, two)


def per_device(queries, keys, values, gate, conv_weight):
    frames, rows, width, channels = queries.shape
    tokens = rows * width
    n_row, n_frame = lax.axis_size("row"), lax.axis_size("frame")
    me_row, me_frame = lax.axis_index("row"), lax.axis_index("frame")
    f32, bf16 = jnp.float32, jnp.bfloat16

    top = n_row // 2
    plan = Plan(channels, 2)
    own = (me_row // top).astype(jnp.int32).reshape(1)
    other = 1 - own

    keys = keys.reshape(frames, tokens, channels)
    values = values.reshape(frames, tokens, channels)
    odd = (me_row % 2).astype(jnp.int32).reshape(1)
    send, mine, far, *near = sums(plan, own, odd, keys, values, queries)
    got = swap(send, "row", top)
    far, forward = cross(far)
    near = [swap(edge, "row", 1) for edge in near]
    mine = mine + got.astype(f32)

    second = (me_frame % 2) == 1
    reaches = [1 << i for i in range((n_frame // 2 - 1).bit_length())]
    once = jnp.minimum(me_frame + 1, 1)

    def arriving(running, reach):
        hop = [(i, i + 2 * reach) for i in range(n_frame - 2 * reach)]
        return lax.ppermute(running, "frame", hop)

    def nearest(_, carry):
        total, moving = carry
        neighbour = swap(moving, "frame", 1).astype(f32)
        before, running = jnp.where(second, neighbour, 0.0), (total + neighbour).astype(bf16)
        for reach in reaches[:1]:
            earlier = arriving(running, reach).astype(f32)
            before, running = before + earlier, (total + neighbour + earlier).astype(bf16)
        return before, running

    def farther(_, carry):
        before, running = carry
        for reach in reaches[1:]:
            earlier = arriving(running, reach)
            before = before + earlier.astype(f32)
            running = (running.astype(f32) + earlier.astype(f32)).astype(bf16)
        return before, running

    total = jnp.sum(mine, axis=0)
    before, running = lax.fori_loop(0, once, nearest, (total, total.astype(bf16)))
    running, far = lax.optimization_barrier((running, far))
    far = forward(far)
    before, _ = lax.fori_loop(0, once, farther, (before, running))
    before, near = lax.optimization_barrier((before, near))
    states = before[None] + jnp.cumsum(mine, axis=0)
    bit = 1
    while bit < top:
        moving = states.astype(bf16)
        if bit == 1:
            moving, queries, gate = lax.optimization_barrier((moving, queries, gate))
            qf, sg = ready(plan, queries, gate)
        arrived = swap(moving, "row", bit)
        if bit == 1:
            arrived, qf, sg = lax.optimization_barrier((arrived, qf, sg))
        states = states + arrived.astype(f32)
        bit *= 2
    states = states.astype(bf16)
    others = swap(states, "row", top)

    shape = queries.shape
    out = mix(plan, shape, own, odd, states, qf, near, far, sg, conv_weight, None)
    return mix(plan, shape, other, odd, others, qf, near, far, sg, conv_weight, out)


def solution(mesh):
    spec = P("frame", "row", None, None)
    return jax.shard_map(
        per_device,
        mesh=mesh,
        in_specs=(spec, spec, spec, spec, P()),
        out_specs=spec,
        check_vma=False,
    )
```
